512 devices in a mesh: island: 64 (over y, x, z_hi, core), fsdp: 8 (over z_lo).
Axes of the slice: x: 4, y: 4, z: 16 (z_hi: 2, z_lo: 8; z = z_hi * 8 + z_lo), core: 2. Of those that a mesh axis runs over, the one named last changes fastest.
Arguments:
- anchor: float32 [8192, 128], P('fsdp'), may hold values from -6 to 6
- inner_drift: float32 [64, 8192, 128], P('island', 'fsdp'), may hold values from -6 to 6
- gradient: bfloat16 [64, 8192, 128], P('island', 'fsdp'), may hold values from -400 to 400
- first_moment: float32 [64, 8192, 128], P('island', 'fsdp'), may hold values from -6 to 6
- second_moment: float32 [64, 8192, 128], P('island', 'fsdp'), may hold values from 0.1 to 4
- outer_momentum: float32 [8192, 128], P('fsdp'), may hold values from -6 to 6
Outputs:
- new_first: float32 [64, 8192, 128], P('island', 'fsdp')
- new_second: float32 [64, 8192, 128], P('island', 'fsdp')
- new_anchor: float32 [8192, 128], P('fsdp')
- new_momentum: float32 [8192, 128], P('fsdp')
The draws below stay inside these ranges and needn't reach their ends.
All inputs are finite; a program needn't handle non-finite values.
Results may differ from the reference program's by a relative error of at most 0.0003.
Values sent between devices are 32-bit elements; how exact they have to be, the bound alone decides.
A program may use at most 64 MiB of HBM per device.

```python
import math
import jax
import jax.numpy as jnp
from jax import lax

LANE = 128
INNER_STEP = 500
ROWS = 8192
N_ISLAND = 64


def draw_gradient(key, part):
    key = jax.random.fold_in(key, 7)
    base_key, column_key, order_key, offset_key = jax.random.split(key, 4)
    position = jnp.arange(ROWS, dtype=jnp.float32) / float(ROWS - 1)
    column_scale = 10.0 ** jax.random.uniform(column_key, (LANE,), jnp.float32)
    order = jax.random.permutation(order_key, N_ISLAND).astype(jnp.float32)
    offset = jax.random.uniform(offset_key, (N_ISLAND,), jnp.float32)
    island_scale = 10.0 ** (-1.5 + 2.0 * (order + offset) / float(N_ISLAND))
    base = jnp.clip(jax.random.normal(base_key, (N_ISLAND, ROWS, LANE), jnp.float32), -4.0, 4.0) * 0.2
    row_scale = 10.0 ** position
    scaled = base * island_scale[:, None, None] * row_scale[None, :, None] * column_scale[None, None, :]
    return scaled.astype(jnp.bfloat16)


def level_of(key, dims, cuts, smallest, high):
    gain = 1.0
    for axis_at, parts in cuts:
        draws = jax.random.uniform(jax.random.fold_in(jax.random.fold_in(key, 6), axis_at), (parts,), jnp.float32, smallest / len(cuts), high / len(cuts))
        gain = gain * jnp.repeat(jnp.exp(draws), dims[axis_at] // parts).reshape((-1,) + (1,) * (len(dims) - 1 - axis_at))
    return gain


def scatter_about(own_key, dims, spread, most, cuts=(), kind=jnp.bfloat16):
    gain = level_of(own_key, dims, cuts, -0.22, 0.18) if cuts else 1.0
    array = jax.random.normal(own_key, dims, jnp.float32) * spread * gain
    return jnp.minimum(jnp.maximum(array, -most), most).astype(kind)


def setup_inputs(seed: int = 0) -> dict:
    arg_keys = jax.random.split(jax.random.key(seed), 7)
    return {
        "anchor": scatter_about(arg_keys[0], (ROWS, LANE), 1.0, 6.0, ((0, 8),), jnp.float32),
        "inner_drift": scatter_about(arg_keys[1], (N_ISLAND, ROWS, LANE), 0.5, 6.0, ((0, 64), (1, 8)), jnp.float32),
        "gradient": draw_gradient(jax.random.fold_in(arg_keys[6], 71), 0),
        "first_moment": scatter_about(arg_keys[3], (N_ISLAND, ROWS, LANE), 0.5, 6.0, ((0, 64), (1, 8)), jnp.float32),
        "second_moment": jnp.clip(jnp.exp(math.log(4.0) - 3.6888794 * jax.random.uniform(arg_keys[4], (N_ISLAND, ROWS, LANE), jnp.float32) ** level_of(arg_keys[4], (N_ISLAND, ROWS, LANE), ((0, 64), (1, 8)), -0.2, 0.2)), 0.1, 4.0),
        "outer_momentum": scatter_about(arg_keys[5], (ROWS, LANE), 0.5, 6.0, ((0, 8),), jnp.float32),
    }


BETA_ONE = 0.9
BETA_TWO = 0.95
adam_epsilon = 1e-08
inner_rate = 0.3
decay_rate = 0.1
outer_rate = 0.7
outer_beta = 0.9

def adam_rows(anchor, drift, gradient, first, second, factor):
    params = anchor + drift
    clipped = gradient.astype(jnp.float32) * factor
    new_first = BETA_ONE * first + (1.0 - BETA_ONE) * clipped
    new_second = BETA_TWO * second + (1.0 - BETA_TWO) * clipped * clipped
    first_fix = 1.0 - BETA_ONE ** INNER_STEP
    second_fix = 1.0 - BETA_TWO ** INNER_STEP
    adam = new_first / first_fix / (jnp.sqrt(new_second / second_fix) + adam_epsilon)
    updated = params - inner_rate * (adam + decay_rate * params)
    return (new_first, new_second, anchor - updated)

def outer_update(anchor, momentum, summed, count):
    average = summed / count
    new_momentum = outer_beta * momentum + average
    new_anchor = anchor - outer_rate * (average + outer_beta * new_momentum)
    return (new_anchor, new_momentum)

def reference(anchor, inner_drift, gradient, first_moment, second_moment, outer_momentum):
    limit = math.sqrt(ROWS * LANE)

    def island_step(total, pieces):
        drift, grads, first, second = pieces
        wide = grads.astype(jnp.float32)
        norm_value = jnp.sqrt(jnp.sum(wide * wide))
        factor = jnp.minimum(1.0, limit / (norm_value + 1e-06))
        new_first, new_second, pseudo = adam_rows(anchor, drift, grads, first, second, factor)
        return (total + pseudo, (new_first, new_second))
    start = jnp.zeros(anchor.shape, jnp.float32)
    total, (new_first, new_second) = lax.scan(island_step, start, (inner_drift, gradient, first_moment, second_moment))
    new_anchor, new_momentum = outer_update(anchor, outer_momentum, total, float(N_ISLAND))
    return (new_first, new_second, new_anchor, new_momentum)
```

```python
import functools
import math

import jax
import jax.numpy as jnp
from jax import lax
from jax.experimental import pallas as pl
from jax.experimental.pallas import tpu as pltpu
from jax.sharding import PartitionSpec as P

INNER_STEP = 500
BETA_ONE = 0.9
BETA_TWO = 0.95
ADAM_EPSILON = 1e-08
INNER_RATE = 0.3
DECAY_RATE = 0.1
OUTER_RATE = 0.7
OUTER_BETA = 0.9

SIDE = 4
PLANE = SIDE * SIDE
MESH = pl.DeviceIdType.MESH


def adam_rows(anchor, drift, gradient, first, second, factor):
    params = anchor + drift
    clipped = gradient.astype(jnp.float32) * factor
    new_first = BETA_ONE * first + (1.0 - BETA_ONE) * clipped
    new_second = BETA_TWO * second + (1.0 - BETA_TWO) * clipped * clipped
    first_fix = 1.0 - BETA_ONE**INNER_STEP
    second_fix = 1.0 - BETA_TWO**INNER_STEP
    adam = new_first / first_fix / (jnp.sqrt(new_second / second_fix) + ADAM_EPSILON)
    updated = params - INNER_RATE * (adam + DECAY_RATE * params)
    return (new_first, new_second, anchor - updated)


def outer_update(anchor, momentum, summed, count):
    average = summed / count
    new_momentum = OUTER_BETA * momentum + average
    new_anchor = anchor - OUTER_RATE * (average + OUTER_BETA * new_momentum)
    return (new_anchor, new_momentum)


def kernel(
    shards, islands, limit,
    anchor_hbm, drift_hbm, grad_hbm, first_hbm, second_hbm, mom_hbm,
    new_first, new_second, na, nm,
    anchor, drift, grad, first, second, mom,
    part, parts, sib_out, own, sib_in, plane_out, plane_in, z_out, z_in, full,
    in_sems, part_send, part_recv, sib_send, sib_recv,
    plane_send, plane_recv, z_send, z_recv, all_send, all_recv, fwd_send, fwd_recv,
):
    rows = anchor.shape[0]
    half = rows // 2
    step = half // PLANE
    island = lax.axis_index("island")
    shard = lax.axis_index("fsdp")
    core = island % 2
    far = (island // 2) % 2
    place = island // 4
    py, px = place // SIDE, place % SIDE

    def spot(r):
        return ((py + r // SIDE) % SIDE) * SIDE + (px + r % SIDE) % SIDE

    def back(r):
        return ((py + SIDE - r // SIDE) % SIDE) * SIDE + (px + SIDE - r % SIDE) % SIDE

    def peer(r):
        return (spot(r) * 4 + far * 2 + core, shard)

    sibling = (place * 4 + far * 2 + (1 - core), shard)
    across = (place * 4 + (1 - far) * 2 + core, shard)

    def mate(k):
        return (island, (shard + k) % shards)

    def span(c, p):
        return pl.ds(pl.multiple_of(c * half + p * step, step), step)

    loads = [
        pltpu.make_async_copy(src, dst, in_sems.at[i])
        for i, (src, dst) in enumerate(
            [(grad_hbm, grad), (first_hbm, first), (second_hbm, second),
             (anchor_hbm, anchor), (drift_hbm, drift), (mom_hbm, mom)])
    ]
    for load in loads:
        load.start()

    barrier = pltpu.get_barrier_semaphore()
    for k in range(1, shards):
        pl.semaphore_signal(barrier, inc=1, device_id=mate(k), device_id_type=MESH)
    pl.semaphore_signal(barrier, inc=1, device_id=across, device_id_type=MESH)
    pl.semaphore_signal(barrier, inc=1, device_id=sibling, device_id_type=MESH)
    for r in range(1, PLANE):
        pl.semaphore_signal(barrier, inc=1, device_id=peer(r), device_id_type=MESH)

    loads[0].wait()
    wide = grad[...].astype(jnp.float32)
    part[...] = jnp.sum((wide * wide).reshape(rows // 8, 8, 128), axis=0)
    pl.semaphore_wait(barrier, shards - 1 + 2 + PLANE - 1)

    def part_copy(k):
        return pltpu.make_async_remote_copy(
            part, parts.at[k], part_send.at[k], part_recv.at[k], device_id=mate(k), device_id_type=MESH)

    for k in range(1, shards):
        part_copy(k).start()
    for load in loads[1:]:
        load.wait()
    total = part[...]
    for k in range(1, shards):
        part_copy(k).wait_recv()
        total = total + parts[k]
    squares = jnp.sum(total)
    factor = jnp.minimum(1.0, limit / (jnp.sqrt(jnp.full((8, 128), squares, jnp.float32)) + 1e-06))
    factor = jnp.concatenate([factor] * (step // 8), axis=0)

    def adam_block(where):
        nf, ns, pseudo = adam_rows(
            anchor[where, :], drift[where, :], grad[where, :], first[where, :], second[where, :], factor)
        new_first[where, :] = nf
        new_second[where, :] = ns
        return pseudo

    def sib_copy(r):
        return pltpu.make_async_remote_copy(
            sib_out.at[r], sib_in.at[r], sib_send.at[r], sib_recv.at[r], device_id=sibling, device_id_type=MESH)

    @pl.loop(1, PLANE + 1)
    def _(i):
        r = i % PLANE
        sib_out[r] = adam_block(span(1 - core, spot(r)))
        sib_copy(r).start()

    @pl.loop(0, PLANE)
    def _(r):
        own[r] = adam_block(span(core, spot(r)))

    def plane_copy(r):
        return pltpu.make_async_remote_copy(
            plane_out.at[r], plane_in.at[r], plane_send.at[r], plane_recv.at[r],
            device_id=peer(r), device_id_type=MESH)

    @pl.loop(1, PLANE)
    def _(r):
        sib_copy(r).wait_recv()
        plane_out[r] = own[r] + sib_in[r]
        plane_copy(r).start()

    sib_copy(0).wait_recv()

    def add(r, acc):
        plane_copy(r).wait_recv()
        return acc + plane_in[r]

    z_out[...] = lax.fori_loop(1, PLANE, add, own[0] + sib_in[0])
    z_copy = pltpu.make_async_remote_copy(
        z_out, z_in, z_send, z_recv, device_id=across, device_id_type=MESH)
    z_copy.start()
    z_copy.wait_recv()
    mine = span(core, place)
    full[mine, :] = z_out[...] + z_in[...]

    def all_copy(r):
        return pltpu.make_async_remote_copy(
            full.at[mine, :], full.at[mine, :], all_send.at[r], all_recv.at[r],
            device_id=peer(r), device_id_type=MESH)

    def fwd_copy(r):
        where = span(core, back(r))
        return pltpu.make_async_remote_copy(
            full.at[where, :], full.at[where, :], fwd_send.at[r], fwd_recv.at[r],
            device_id=sibling, device_id_type=MESH)

    @pl.loop(1, PLANE)
    def _(r):
        all_copy(r).start()

    fwd_copy(0).start()

    def outer_block(where):
        na[where, :], nm[where, :] = outer_update(anchor[where, :], mom[where, :], full[where, :], islands)

    outer_block(mine)

    @pl.loop(1, PLANE)
    def _(r):
        where = span(core, back(r))
        pltpu.make_async_remote_copy(
            full.at[where, :], full.at[where, :], all_send.at[r], all_recv.at[r],
            device_id=peer(r), device_id_type=MESH).wait_recv()
        fwd_copy(r).start()
        outer_block(where)

    @pl.loop(0, PLANE)
    def _(r):
        where = span(1 - core, back(r))
        pltpu.make_async_remote_copy(
            full.at[where, :], full.at[where, :], fwd_send.at[r], fwd_recv.at[r],
            device_id=sibling, device_id_type=MESH).wait_recv()
        outer_block(where)

    for k in range(1, shards):
        part_copy(k).wait_send()
    z_copy.wait_send()

    @pl.loop(1, PLANE)
    def _(r):
        sib_copy(r).wait_send()
        plane_copy(r).wait_send()
        all_copy(r).wait_send()
        fwd_copy(r).wait_send()

    sib_copy(0).wait_send()
    fwd_copy(0).wait_send()


def write_out(*refs):
    sources, targets, sems = refs[:4], refs[4:8], refs[8]
    copies = [pltpu.make_async_copy(s, t, sems.at[i]) for i, (s, t) in enumerate(zip(sources, targets))]
    for copy in copies:
        copy.start()
    for copy in copies:
        copy.wait()


def per_device(anchor, inner_drift, gradient, first_moment, second_moment, outer_momentum):
    rows, lanes = anchor.shape
    shards = lax.axis_size("fsdp")
    islands = float(lax.axis_size("island"))
    limit = math.sqrt(shards * rows * lanes)
    step = rows // 2 // PLANE
    f32 = jnp.float32
    whole = pltpu.VMEM((rows, lanes), f32)
    blocks = pltpu.VMEM((PLANE, step, lanes), f32)
    block = pltpu.VMEM((step, lanes), f32)
    dma = pltpu.SemaphoreType.DMA
    hbm = pl.BlockSpec(memory_space=pltpu.HBM)
    vmem = pl.BlockSpec(memory_space=pltpu.VMEM)
    results = pl.pallas_call(
        functools.partial(kernel, shards, islands, limit),
        out_shape=[pltpu.VMEM((rows, lanes), f32)] * 4,
        in_specs=[hbm] * 6,
        out_specs=[vmem] * 4,
        scratch_shapes=[
            whole, whole, pltpu.VMEM((rows, lanes), jnp.bfloat16), whole, whole, whole,
            pltpu.VMEM((8, lanes), f32), pltpu.VMEM((shards, 8, lanes), f32),
            blocks, blocks, blocks, blocks, blocks, block, block, whole,
            dma((6,)), dma((shards,)), dma((shards,)), dma((PLANE,)), dma((PLANE,)),
            dma((PLANE,)), dma((PLANE,)), dma, dma, dma((PLANE,)), dma((PLANE,)), dma((PLANE,)), dma((PLANE,)),
        ],
        compiler_params=pltpu.CompilerParams(
            collective_id=0, has_side_effects=True, vmem_limit_bytes=60 * 1024 * 1024),
        cost_estimate=pl.CostEstimate(flops=40 * rows * lanes, bytes_accessed=40 * rows * lanes, transcendentals=0),
    )(anchor, inner_drift[0], gradient[0], first_moment[0], second_moment[0], outer_momentum)
    nf, ns, na, nm = pl.pallas_call(
        write_out,
        out_shape=[jax.ShapeDtypeStruct((rows, lanes), f32)] * 4,
        in_specs=[pl.BlockSpec(memory_space=pl.ANY)] * 4,
        out_specs=[hbm] * 4,
        scratch_shapes=[dma((4,))],
        compiler_params=pltpu.CompilerParams(vmem_limit_bytes=1024 * 1024),
        cost_estimate=pl.CostEstimate(flops=0, bytes_accessed=16 * rows * lanes, transcendentals=0),
    )(*results)
    return (nf[None], ns[None], na, nm)


def solution(mesh):
    return jax.shard_map(
        per_device,
        mesh=mesh,
        in_specs=(
            P("fsdp", None),
            P("island", "fsdp", None),
            P("island", "fsdp", None),
            P("island", "fsdp", None),
            P("island", "fsdp", None),
            P("fsdp", None),
        ),
        out_specs=(
            P("island", "fsdp", None),
            P("island", "fsdp", None),
            P("fsdp", None),
            P("fsdp", None),
        ),
        check_vma=False,
    )
```
